32 devices in a mesh: dp: 4 (over z), expert: 4 (over y, x), pair: 2 (over core).
Axes of the slice: x: 2, y: 2, z: 4, core: 2. Of those that a mesh axis runs over, the one named last changes fastest.
Arguments:
- tokens: bfloat16 [2048, 2048], P(('dp', 'expert'), 'pair'), may hold values from -6 to 6
- grad_out: bfloat16 [2048, 2048], P(('dp', 'expert'), 'pair'), may hold values from -6 to 6
- routes: int32 [2048, 2], P(('dp', 'expert')), may hold values from 0 to 3, all different within a row; in each aligned block of 128 rows (0 to 127, 128 to 255, ...) at most 96 rows name the same one
- gate_probs: float32 [2048, 2], P(('dp', 'expert')), may hold values from 0.1 to 1
- gate_weight: bfloat16 [4, 2048, 768], P('expert', None, 'pair'), may hold values from -0.125 to 0.125
- up_weight: bfloat16 [4, 2048, 768], P('expert', None, 'pair'), may hold values from -0.125 to 0.125
- down_weight: bfloat16 [4, 768, 2048], P('expert', 'pair'), may hold values from -0.21875 to 0.21875
Outputs:
- grad_input: bfloat16 [2048, 2048], P(('dp', 'expert'), 'pair')
- grad_probs: float32 [2048, 2], P(('dp', 'expert'))
- grad_down: float32 [4, 2048, 768], P('expert', 'dp', 'pair')
The draws below stay inside these ranges and needn't reach their ends.
Inputs may be any that keep to these rules, and one draw needn't show every extreme that they name: `routes`: each row names 2 different experts. In each aligned block of 128 rows (the tokens of one device) no expert is named by more than 96 rows, a bound that some block reaches.
All inputs are finite; a program needn't handle non-finite values.
Results may differ from the reference program's by a relative error of at most 0.02.
Values may be sent and summed in bfloat16 or wider, within the bound.
No kernel may reach another device: no remote copies, remote signals or barrier semaphores. Data moves between devices by JAX's collectives and lax.ppermute only.
A program may use at most 64 MiB of HBM per device.

```python
import math
import jax
import jax.numpy as jnp
import numpy as np
from jax import lax

D = 2048
FF = 768
TOK_DEV = 128
TOP = 2
EXPERTS = 4
CAP = 96
TOKENS = 2048
N_PAIR = 2


def with_spikes(array, stream_key, source, target, shards_of, factor):
    owner, partner = [(jnp.arange(array.shape[axis_at]) // (array.shape[axis_at] // shards_of)).reshape([-1 if axis == axis_at else 1 for axis in range(array.ndim)]) for axis_at in (source, target)]
    chosen = jax.random.permutation(stream_key, shards_of)[partner]
    strong = (owner == chosen) | (owner == (partner + shards_of // 2) % shards_of)
    return jnp.where(strong, factor * array, array)


def block_levels(stream_key, dims, split, least, largest):
    def one(dim, parts):
        draws = jax.random.uniform(jax.random.fold_in(jax.random.fold_in(stream_key, 6), dim), (parts,), jnp.float32, least / len(split), largest / len(split))
        return jnp.repeat(jnp.exp(draws), dims[dim] // parts).reshape((-1,) + (1,) * (len(dims) - dim - 1))

    gain = one(*split[0])
    for cut in split[1:]:
        gain = gain * one(*cut)
    return gain


def deal_out(own_key, own, number, rows, number_of, top, reach, skew):
    ranking = jax.random.permutation(own_key, number_of)
    packed, usual = shares(number_of, rows * top, reach, skew, True), shares(number_of, rows * top, reach, skew, False)
    places = jnp.arange(number_of)

    def named(sizes, turn):
        used = int((sizes > 0).sum())
        fixed = max(1, used // 4)
        moved = fixed + (places - fixed + turn * (used - fixed)) % max(1, number_of - fixed)
        return jnp.zeros((number_of,), jnp.int32).at[ranking[jnp.where(places < fixed, places, moved)]].set(jnp.asarray(sizes, jnp.int32))

    sizes = jnp.where(number % 4 == 0, named(packed, number // 4), named(usual, number - number // 4 - 1))
    mixed = jax.random.permutation(jax.random.fold_in(own, 3), number_of)
    source_of, taker = mixed[0:number_of // 2 * 2:2], mixed[1:number_of // 2 * 2:2]
    slack = jnp.minimum(sizes[source_of] - 1, reach - sizes[taker]) // 2
    slack = jnp.where((source_of == ranking[0]) | (taker == ranking[0]) | (sizes[taker] == 0), 0, jnp.maximum(slack, 0))
    moved = jax.random.randint(jax.random.fold_in(own, 4), (number_of // 2,), 0, 1 << 20) % (slack + 1)
    sizes = sizes.at[source_of].add(-moved).at[taker].add(moved)
    labels = jnp.searchsorted(jnp.cumsum(sizes), jnp.arange(rows * top), side="right").astype(jnp.int32)
    listing = labels.reshape(top, rows).T
    listing = listing[jax.random.permutation(jax.random.fold_in(own, 1), rows)]
    turn = jax.random.randint(jax.random.fold_in(own, 2), (rows, 1), 0, top)
    return jnp.take_along_axis(listing, (jnp.arange(top)[None, :] + turn) % top, axis=1)


def shares(count, total, limit, skew, full):
    portions = [(1 << 20) // math.isqrt(grade ** skew) + 1 for grade in range(1, count + 1)]
    largest = limit if full else min(limit, max(-(-total // count), total * portions[0] // sum(portions)))
    least = 1 if total - largest >= count - 1 else 0
    given, spare = [largest] + [least] * (count - 1), total - largest - least * (count - 1)
    while spare > 0:
        free = [i for i in range(1, count) if given[i] < largest] or [i for i in range(1, count) if given[i] < limit]
        mass, remaining = sum([portions[i] for i in free]), spare
        for i in free:
            extra = min(limit - given[i], max(1, remaining * portions[i] // mass), spare)
            given[i] = given[i] + extra
            spare = spare - extra
    return np.array(given)


def normal_values(own_key, extent, spread, limit, split=(), kind=jnp.bfloat16):
    array = spread * jax.random.normal(own_key, extent, jnp.float32)
    if split:
        array = array * block_levels(own_key, extent, split, -0.22, 0.18)
    return jnp.clip(array, -limit, limit).astype(kind)


def gaussian_with(own_key, dims, scale, bound, split, heavy, held_as=jnp.bfloat16):
    array = scale * jax.random.normal(own_key, dims, jnp.float32)
    if split:
        array = array * block_levels(own_key, dims, split, -0.22, 0.18)
    return jnp.clip(with_spikes(array, jax.random.fold_in(own_key, 3), *heavy), -bound, bound).astype(held_as)


def setup_inputs(seed: int = 0) -> dict:
    keys = jax.random.split(jax.random.key(seed), 8)
    tokens = normal_values(keys[0], (TOKENS, D), 1.0, 6.0, ((0, 16), (1, 2)))
    grad_out = gaussian_with(keys[1], (TOKENS, D), 1.0, 6.0, ((0, 16), (1, 2)), (0, 1, 16, 2.0))
    routes_keys = jax.random.split(jax.random.fold_in(keys[2], 1), TOKENS // TOK_DEV)
    routes_turns = jax.random.permutation(jax.random.fold_in(keys[2], 3), TOKENS // TOK_DEV)
    routes = jax.vmap(lambda own, number: deal_out(jax.random.fold_in(keys[2], 2), own, number, TOK_DEV, EXPERTS, TOP, CAP, 1))(routes_keys, routes_turns).reshape((TOKENS, TOP))
    gate_probs = jnp.clip(0.1 + 0.9 * jax.random.uniform(keys[3], (TOKENS, TOP), jnp.float32) ** block_levels(keys[3], (TOKENS, TOP), ((0, 16),), -0.2, 0.2), 0.1, 1.0)
    gate_weight = normal_values(keys[4], (EXPERTS, D, FF), D ** -0.5, 0.125, ((0, 4), (2, 2)))
    up_weight = normal_values(keys[5], (EXPERTS, D, FF), D ** -0.5, 0.125, ((0, 4), (2, 2)))
    down_weight = normal_values(keys[6], (EXPERTS, FF, D), FF ** -0.5, 0.21875, ((0, 4), (1, 2)))
    return dict(tokens=tokens, grad_out=grad_out, routes=routes, gate_probs=gate_probs, gate_weight=gate_weight, up_weight=up_weight, down_weight=down_weight)


def reference(tokens, grad_out, routes, gate_probs, gate_weight, up_weight, down_weight):
    block_count = TOKENS // TOK_DEV
    expert_ids = jnp.arange(EXPERTS, dtype=jnp.int32)
    hits = jnp.sum((routes[:, :, None] == expert_ids[None, None, :]).astype(jnp.int32), axis=1)
    blocked = hits.reshape(block_count, TOK_DEV, EXPERTS)
    before = (jnp.cumsum(blocked, axis=1) - blocked).reshape(TOKENS, EXPERTS)
    position = jnp.take_along_axis(before, routes, axis=1)
    owner = (jnp.arange(TOKENS, dtype=jnp.int32) // TOK_DEV)[:, None]
    placed = (owner * CAP + position).astype(jnp.int32)
    span = block_count * CAP
    half_units = FF // N_PAIR

    def one_expert(carry, index):
        grad_in, grad_pr = carry
        chosen_mask = routes == index
        chosen = jnp.any(chosen_mask, axis=1)
        where_to = jnp.where(chosen, jnp.sum(jnp.where(chosen_mask, placed, 0), axis=1), span).astype(jnp.int32)
        weight_tok = jnp.sum(jnp.where(chosen_mask, gate_probs, 0.0), axis=1)
        inputs = jnp.zeros((span, D), jnp.bfloat16).at[where_to].set(tokens, mode="drop")
        upstream = jnp.zeros((span, D), jnp.bfloat16).at[where_to].set(grad_out, mode="drop")
        weight_row = jnp.zeros((span,), jnp.float32).at[where_to].set(weight_tok, mode="drop")
        gate_mat = gate_weight[index]
        up_mat = up_weight[index]
        down_mat = down_weight[index]
        gate_pre = jnp.dot(inputs, gate_mat, preferred_element_type=jnp.float32)
        up_pre = jnp.dot(inputs, up_mat, preferred_element_type=jnp.float32)
        sigma = jax.nn.sigmoid(gate_pre)
        active = gate_pre * sigma
        hidden = active * up_pre
        back = jnp.dot(upstream, down_mat.T, preferred_element_type=jnp.float32)
        prob_part = jnp.sum(hidden * back, axis=1)
        scaled = (weight_row[:, None] * upstream.astype(jnp.float32)).astype(jnp.bfloat16)
        weight_term = jnp.dot(scaled.T, hidden.astype(jnp.bfloat16), preferred_element_type=jnp.float32)
        grad_hidden = weight_row[:, None] * back
        grad_gate = (grad_hidden * up_pre * sigma * (1.0 + gate_pre * (1.0 - sigma))).astype(jnp.bfloat16)
        grad_up = (grad_hidden * active).astype(jnp.bfloat16)
        slot_grad = jnp.zeros((span, D), jnp.float32)
        for half in range(N_PAIR):
            low = half * half_units
            term = jnp.dot(grad_gate[:, low:low + half_units], gate_mat[:, low:low + half_units].T, preferred_element_type=jnp.float32)
            term = term + jnp.dot(grad_up[:, low:low + half_units], up_mat[:, low:low + half_units].T, preferred_element_type=jnp.float32)
            slot_grad = slot_grad + term.astype(jnp.bfloat16).astype(jnp.float32)
        grad_in = grad_in + jnp.take(slot_grad, where_to, axis=0, mode="fill", fill_value=0.0)
        taken = jnp.take(prob_part, where_to, axis=0, mode="fill", fill_value=0.0)
        grad_pr = grad_pr + jnp.where(chosen_mask, taken[:, None], 0.0)
        return (grad_in, grad_pr), weight_term

    start = (jnp.zeros((TOKENS, D), jnp.float32), jnp.zeros((TOKENS, TOP), jnp.float32))
    (grad_in, grad_pr), grad_down = lax.scan(one_expert, start, expert_ids)
    return grad_in.astype(jnp.bfloat16), grad_pr, grad_down
```

```python
import functools

import jax
import jax.numpy as jnp
from jax import lax
from jax.experimental import pallas as pl
from jax.experimental.pallas import tpu as pltpu
from jax.sharding import PartitionSpec as P

F32 = jnp.float32
BF16 = jnp.bfloat16
NT = (((1,), (1,)), ((), ()))
TN = (((0,), (0,)), ((), ()))
VMEM_LIMIT = 48 * 1024 * 1024


def dot(a, b, dims=(((1,), (0,)), ((), ()))):
    return lax.dot_general(a, b, dims, preferred_element_type=F32)


def call(body, out_shape, operands, scalars=None):
    in_specs = [pl.BlockSpec(memory_space=pltpu.VMEM)] * len(operands)
    if scalars is not None:
        operands = [scalars] + list(operands)
        in_specs = [pl.BlockSpec(memory_space=pltpu.SMEM)] + in_specs
    return pl.pallas_call(
        body,
        out_shape=out_shape,
        in_specs=in_specs,
        out_specs=jax.tree.map(lambda _: pl.BlockSpec(memory_space=pltpu.VMEM), out_shape),
        compiler_params=pltpu.CompilerParams(vmem_limit_bytes=VMEM_LIMIT),
    )(*operands)


def struct(shape, dtype):
    return jax.ShapeDtypeStruct(shape, dtype)


def pack_body(experts, cap, sc, routes_ref, probs_ref, tok_ref, dy_ref, *outs):
    x_out, a_out, b_out, s_out = outs[:experts], outs[experts:2 * experts], outs[2 * experts:3 * experts], outs[3 * experts]
    me, pair = sc[0], sc[1]
    fanout, count = routes_ref.shape
    half = dy_ref.shape[1] // 2
    off_a = pl.multiple_of(pair * half, half)
    off_b = pl.multiple_of((1 - pair) * half, half)
    routes = routes_ref[...]
    probs = probs_ref[...]
    row = lax.broadcasted_iota(jnp.int32, (8, count), 0)
    hits = jnp.zeros((8, count), F32)
    weights = jnp.zeros((8, count), F32)
    for k in range(fanout):
        same = routes[k:k + 1, :] == (row ^ me)
        hits = hits + jnp.where(same, 1.0, 0.0)
        weights = weights + jnp.where(same, probs[k:k + 1, :], 0.0)
    earlier = lax.broadcasted_iota(jnp.int32, (count, count), 0) < lax.broadcasted_iota(jnp.int32, (count, count), 1)
    before = dot(hits.astype(BF16), jnp.where(earlier, 1.0, 0.0).astype(BF16)).astype(jnp.int32)
    slot = lax.broadcasted_iota(jnp.int32, (cap, count), 0)
    tok = tok_ref[...]
    for m in range(experts):
        chosen = (slot == before[m:m + 1, :]) & (hits[m:m + 1, :] > 0.5)
        pick = jnp.where(chosen, 1.0, 0.0)
        pick_b = pick.astype(BF16)
        s_out[m * cap:(m + 1) * cap, :] = pick_b
        x_out[m][...] = dot(pick_b, tok).astype(BF16)
        p_col = jnp.sum(pick * weights[m:m + 1, :], axis=1, keepdims=True)
        a_out[m][...] = (p_col * dot(pick_b, dy_ref[:, pl.ds(off_a, half)])).astype(BF16)
        b_out[m][...] = (p_col * dot(pick_b, dy_ref[:, pl.ds(off_b, half)])).astype(BF16)


def rows_of(refs):
    return jnp.concatenate([r[...] for r in refs], axis=0)


def forward_body(experts, sc, *refs):
    own, oth = refs[:experts], refs[experts:2 * experts]
    gw, uw, hid_ref, hid_b_ref, dgate_ref, act_ref = refs[2 * experts:]
    pair = sc[1]
    half = own[0].shape[1]
    mine = pl.ds(pl.multiple_of(pair * half, half), half)
    other = pl.ds(pl.multiple_of((1 - pair) * half, half), half)
    x_own, x_oth = rows_of(own), rows_of(oth)
    gate = dot(x_own, gw[mine, :]) + dot(x_oth, gw[other, :])
    up = dot(x_own, uw[mine, :]) + dot(x_oth, uw[other, :])
    sig = jax.nn.sigmoid(gate)
    act = gate * sig
    hid = act * up
    hid_ref[...] = hid
    hid_b_ref[...] = hid.astype(BF16)
    dgate_ref[...] = up * sig * (1.0 + gate * (1.0 - sig))
    act_ref[...] = act


def weight_body(experts, flag_at, want, sc, *refs):
    own, oth = refs[:experts], refs[experts:2 * experts]
    hid_b, out = refs[2 * experts:]
    use_own = sc[flag_at] == want

    @pl.when(use_own)
    def _():
        out[...] = dot(rows_of(own), hid_b[...], TN).astype(out.dtype)

    @pl.when(jnp.logical_not(use_own))
    def _():
        out[...] = dot(rows_of(oth), hid_b[...], TN).astype(out.dtype)


def backward_body(experts, sc, *refs):
    a_own, a_oth, b_own, b_oth = (refs[i * experts:(i + 1) * experts] for i in range(4))
    dw, gw, uw, hid_ref, dgate_ref, act_ref, keep_ref, send_ref, q_ref = refs[4 * experts:]
    pair = sc[1]
    quarter = a_own[0].shape[1]
    half = 2 * quarter

    def cols(index):
        return pl.ds(pl.multiple_of(index * quarter, quarter), quarter)

    back = dot(rows_of(a_own), dw[:, cols(3 * pair)], NT)
    back = back + dot(rows_of(a_oth), dw[:, cols(3 - 3 * pair)], NT)
    back = back + dot(rows_of(b_own), dw[:, cols(1 + pair)], NT)
    back = back + dot(rows_of(b_oth), dw[:, cols(2 - pair)], NT)
    g_gate = (back * dgate_ref[...]).astype(BF16)
    g_up = (back * act_ref[...]).astype(BF16)
    q = jnp.sum(back * hid_ref[...], axis=1, keepdims=True)
    other = pl.ds(pl.multiple_of((1 - pair) * half, half), half)
    mine = pl.ds(pl.multiple_of(pair * half, half), half)
    send_ref[:, :half] = (dot(g_gate, gw[other, :], NT) + dot(g_up, uw[other, :], NT)).astype(BF16)
    send_ref[:, half:] = split_columns(q)
    keep_ref[...] = (dot(g_gate, gw[mine, :], NT) + dot(g_up, uw[mine, :], NT)).astype(BF16)
    q_ref[...] = jnp.broadcast_to(q, q_ref.shape)


def split_columns(q):
    high = q.astype(BF16)
    low = (q - high.astype(F32)).astype(BF16)
    lane = lax.broadcasted_iota(jnp.int32, (q.shape[0], 128), 1)
    return jnp.where(lane == 0, high.astype(F32), jnp.where(lane == 1, low.astype(F32), 0.0)).astype(BF16)


def merge_body(experts, keep_ref, q_ref, recv_ref, *outs):
    cap, wide = outs[0].shape
    half = wide - 128
    for m in range(experts):
        rows = slice(m * cap, (m + 1) * cap)
        outs[m][:, :half] = (keep_ref[rows, :].astype(F32) + recv_ref[rows, :half].astype(F32)).astype(BF16)
        tail = recv_ref[rows, half:].astype(F32)
        outs[m][:, half:] = split_columns(q_ref[rows, 0:1] + tail[:, 0:1] + tail[:, 1:2])


def combine_body(experts, sc, pick_ref, routes_ref, probs_ref, *refs):
    parts, (out, gp_out) = refs[:experts], refs[experts:]
    cap, wide = parts[0].shape
    half = wide - 128
    me = sc[0]
    routes = routes_ref[...]
    total = None
    gp = jnp.zeros(gp_out.shape, F32)
    for m in range(experts):
        rows = dot(pick_ref[m * cap:(m + 1) * cap, :], parts[m][...], TN)
        total = rows[:, :half] if total is None else total + rows[:, :half]
        q = rows[:, half:half + 1] + rows[:, half + 1:half + 2]
        gp = gp + jnp.where(routes == (me ^ m), q, 0.0)
    out[...] = total.astype(BF16)
    gp_out[...] = gp / probs_ref[...]


def on_device(tokens, grad_out, routes, gate_probs, gate_weight, up_weight, down_weight):
    count, half = tokens.shape
    fanout = routes.shape[1]
    experts = lax.axis_size("expert")
    groups = lax.axis_size("dp")
    units = gate_weight.shape[2]
    cap = 3 * count * fanout // (2 * experts)
    slots = experts * cap
    quarter = half // 2
    gw, uw, dw = gate_weight[0], up_weight[0], down_weight[0]
    me, pair, group = lax.axis_index("expert"), lax.axis_index("pair"), lax.axis_index("dp")
    scalars = jnp.stack([me, pair, (group + pair) % 2]).astype(jnp.int32)

    def swap(value):
        return lax.ppermute(value, "pair", [(0, 1), (1, 0)])

    def cross(values):
        return [values[0]] + [
            lax.ppermute(values[m], "expert", [(i, i ^ m) for i in range(experts)]) for m in range(1, experts)
        ]

    packed = call(
        functools.partial(pack_body, experts, cap),
        [struct((cap, half), BF16)] * experts
        + [struct((cap, quarter), BF16)] * (2 * experts)
        + [struct((slots, count), BF16)],
        [routes.T, gate_probs.T, tokens, grad_out],
        scalars,
    )
    x_send, a_send, b_send = packed[:experts], packed[experts:2 * experts], packed[2 * experts:3 * experts]
    pick = packed[3 * experts]

    x_own = cross(x_send)
    a_own = cross(a_send)
    b_own = cross(b_send)
    x_oth = [swap(v) for v in x_own]
    a_oth = [swap(v) for v in a_own]
    b_oth = [swap(v) for v in b_own]

    square = struct((slots, units), F32)
    hid, hid_b, dgate, act = call(
        functools.partial(forward_body, experts),
        [square, struct((slots, units), BF16), square, square],
        [*x_own, *x_oth, gw, uw],
        scalars,
    )

    def block(own, oth, want, dtype):
        return call(
            functools.partial(weight_body, experts, 2, want),
            struct((2 * quarter // 2, units), dtype),
            [*own, *oth, hid_b],
            scalars,
        )

    if groups == 4:
        first = block(a_own, a_oth, 1, BF16)
        from_near = lax.ppermute(first, "dp", [(0, 1), (1, 0), (2, 3), (3, 2)])
        a_rest = block(a_own, a_oth, 0, F32)
        second = block(b_own, b_oth, 0, BF16)
        b_rest = block(b_own, b_oth, 1, F32)
        from_mid = lax.ppermute(second, "dp", [(1, 2), (2, 1)])
        from_end = lax.ppermute(second, "dp", [(0, 1), (3, 2)])
        inner = (group == 1) | (group == 2)
        third = jnp.where(inner, a_rest + from_near.astype(F32), b_rest).astype(BF16)
        from_far = lax.ppermute(third, "dp", [(0, 2), (2, 0), (1, 3), (3, 1)])
        grad_down = jnp.where(
            inner,
            b_rest + from_mid.astype(F32) + from_end.astype(F32),
            a_rest + from_near.astype(F32),
        ) + from_far.astype(F32)
        grad_down = grad_down[None]
    else:
        a_one, a_two = block(a_own, a_oth, 1, F32), block(a_own, a_oth, 0, F32)
        b_one, b_two = block(b_own, b_oth, 0, F32), block(b_own, b_oth, 1, F32)
        odd = group % 2 == 1
        whole = jnp.concatenate(
            [
                jnp.where(odd, a_one, a_two),
                jnp.where(odd, b_two, b_one),
                jnp.where(odd, b_one, b_two),
                jnp.where(odd, a_two, a_one),
            ],
            axis=0,
        )
        grad_down = lax.psum_scatter(whole[None], "dp", scatter_dimension=1, tiled=True)

    keep, send, q_own = call(
        functools.partial(backward_body, experts),
        [struct((slots, half), BF16), struct((slots, half + 128), BF16), struct((slots, 128), F32)],
        [*a_own, *a_oth, *b_own, *b_oth, dw, gw, uw, hid, dgate, act],
        scalars,
    )
    merged = call(
        functools.partial(merge_body, experts),
        [struct((cap, half + 128), BF16)] * experts,
        [keep, q_own, swap(send)],
    )
    returned = cross(merged)
    grad_input, grad_probs = call(
        functools.partial(combine_body, experts),
        [struct((count, half), BF16), struct((count, fanout), F32)],
        [pick, routes, gate_probs, *returned],
        scalars,
    )
    return grad_input, grad_probs, grad_down


def solution(mesh):
    return jax.shard_map(
        on_device,
        mesh=mesh,
        in_specs=(
            P(("dp", "expert"), "pair"),
            P(("dp", "expert"), "pair"),
            P(("dp", "expert"), None),
            P(("dp", "expert"), None),
            P("expert", None, "pair"),
            P("expert", None, "pair"),
            P("expert", "pair", None),
        ),
        out_specs=(
            P(("dp", "expert"), "pair"),
            P(("dp", "expert"), None),
            P("expert", "dp", "pair"),
        ),
        check_vma=False,
    )
```

```python
import functools

import jax
import jax.numpy as jnp
from jax import lax
from jax.experimental import pallas as pl
from jax.experimental.pallas import tpu as pltpu
from jax.sharding import PartitionSpec as P

F32 = jnp.float32
BF16 = jnp.bfloat16
NT = (((1,), (1,)), ((), ()))
TN = (((0,), (0,)), ((), ()))
VMEM_LIMIT = 20 * 1024 * 1024
PACK_VMEM = 60 * 1024 * 1024


def dot(a, b, dims=(((1,), (0,)), ((), ()))):
    return lax.dot_general(a, b, dims, preferred_element_type=F32)


def call(body, out_shape, operands, scalars=None, after=(), hbm=(), scratch=(), vmem=VMEM_LIMIT):
    vm = pl.BlockSpec(memory_space=pltpu.VMEM)
    lead = 0 if scalars is None else 1
    specs = [pl.BlockSpec(memory_space=pltpu.SMEM)] * lead
    specs += [pl.BlockSpec(memory_space=pl.ANY)] * len(after)
    specs += [pl.BlockSpec(memory_space=pltpu.HBM) if i in hbm else vm for i in range(len(operands))]

    def run(*refs):
        body(*refs[:lead], *refs[lead + len(after):])

    return pl.pallas_call(
        run,
        out_shape=out_shape,
        in_specs=specs,
        out_specs=jax.tree.map(lambda _: vm, out_shape),
        scratch_shapes=list(scratch),
        compiler_params=pltpu.CompilerParams(vmem_limit_bytes=vmem),
    )(*([] if scalars is None else [scalars]), *after, *operands)


def struct(shape, dtype):
    return jax.ShapeDtypeStruct(shape, dtype)


def slot_rows(experts, me, routes_ref, probs_ref):
    fanout, count = routes_ref.shape
    routes = routes_ref[...]
    probs = probs_ref[...]
    row = lax.broadcasted_iota(jnp.int32, (8, count), 0)
    hits = jnp.zeros((8, count), F32)
    weights = jnp.zeros((8, count), F32)
    for k in range(fanout):
        same = routes[k:k + 1, :] == (row ^ me)
        hits = hits + jnp.where(same, 1.0, 0.0)
        weights = weights + jnp.where(same, probs[k:k + 1, :], 0.0)
    earlier = lax.broadcasted_iota(jnp.int32, (count, count), 0) < lax.broadcasted_iota(jnp.int32, (count, count), 1)
    before = dot(hits.astype(BF16), jnp.where(earlier, 1.0, 0.0).astype(BF16)).astype(jnp.int32)
    return hits, before, weights


def picks(experts, cap, me, routes_ref, probs_ref):
    hits, before, weights = slot_rows(experts, me, routes_ref, probs_ref)
    slot = lax.broadcasted_iota(jnp.int32, (cap, hits.shape[1]), 0)
    found = []
    for m in range(experts):
        chosen = (slot == before[m:m + 1, :]) & (hits[m:m + 1, :] > 0.5)
        pick = jnp.where(chosen, 1.0, 0.0)
        found.append((pick.astype(BF16), jnp.sum(pick * weights[m:m + 1, :], axis=1, keepdims=True)))
    return found


def pack_body(experts, cap, sc, routes_hbm, probs_hbm, tok_hbm, dy_hbm, *rest):
    x_out, dy_out = rest[:experts], rest[experts:2 * experts]
    routes_ref, probs_ref, tok_ref, dy_ref, sems = rest[2 * experts:]
    copies = [
        pltpu.make_async_copy(source, target, sems.at[i])
        for i, (source, target) in enumerate(
            [(routes_hbm, routes_ref), (probs_hbm, probs_ref), (tok_hbm, tok_ref), (dy_hbm, dy_ref)]
        )
    ]
    for copy in copies:
        copy.start()
    copies[0].wait()
    copies[1].wait()
    found = picks(experts, cap, sc[0], routes_ref, probs_ref)
    copies[2].wait()
    tok = tok_ref[...]
    for m, (pick, _) in enumerate(found):
        x_out[m][...] = dot(pick, tok).astype(BF16)
    copies[3].wait()
    dy = dy_ref[...]
    for m, (pick, p_col) in enumerate(found):
        dy_out[m][...] = (p_col * dot(pick, dy)).astype(BF16)


def stack_body(count, *refs):
    blocks, outs = refs[:count], refs[count:]
    cap = blocks[0].shape[0]
    for m, ref in enumerate(blocks):
        rows = slice(m * cap, (m + 1) * cap)
        low = 0
        for out in outs:
            out[rows, :] = ref[:, low:low + out.shape[1]]
            low += out.shape[1]


def forward_body(sc, own, oth, gw, uw, hid_ref, hid_b_ref, dgate_ref, act_ref):
    pair = sc[1]
    half = own.shape[1]
    mine = pl.ds(pl.multiple_of(pair * half, half), half)
    other = pl.ds(pl.multiple_of((1 - pair) * half, half), half)
    gate = dot(own[...], gw[mine, :]) + dot(oth[...], gw[other, :])
    up = dot(own[...], uw[mine, :]) + dot(oth[...], uw[other, :])
    sig = jax.nn.sigmoid(gate)
    act = gate * sig
    hid = act * up
    hid_ref[...] = hid
    hid_b_ref[...] = hid.astype(BF16)
    dgate_ref[...] = up * sig * (1.0 + gate * (1.0 - sig))
    act_ref[...] = act


def weight_body(sc, own, oth, hid_b, first, second, third, fourth):
    group, pair = sc[2], sc[1]
    quarter = own.shape[1] // 2
    odd = group % 2
    hid = hid_b[...]

    def block(out, mine, index):
        columns = pl.ds(pl.multiple_of(index * quarter, quarter), quarter)

        @pl.when(mine)
        def _():
            out[...] = dot(own[:, columns], hid, TN).astype(out.dtype)

        @pl.when(jnp.logical_not(mine))
        def _():
            out[...] = dot(oth[:, columns], hid, TN).astype(out.dtype)

    same = pair == odd
    differ = jnp.logical_not(same)
    block(first, differ, 1 - odd)
    block(second, same, 1 - odd)
    block(third, same, odd)
    block(fourth, differ, odd)


def onward_body(sc, third, fourth, near, out):
    inner = (sc[2] == 1) | (sc[2] == 2)

    @pl.when(inner)
    def _():
        out[...] = (third[...] + near[...].astype(F32)).astype(BF16)

    @pl.when(jnp.logical_not(inner))
    def _():
        out[...] = fourth[...].astype(BF16)


def partial_body(sc, third, fourth, near, end, mid, out):
    inner = (sc[2] == 1) | (sc[2] == 2)

    @pl.when(inner)
    def _():
        out[...] = fourth[...] + mid[...].astype(F32) + end[...].astype(F32)

    @pl.when(jnp.logical_not(inner))
    def _():
        out[...] = third[...] + near[...].astype(F32)


def total_body(part, far, out):
    out[...] = part[...] + far[...].astype(F32)


def backward_body(sc, own, oth, dw, gw, uw, hid_ref, dgate_ref, act_ref, send_ref, grads_ref):
    pair = sc[1]
    units = hid_ref.shape[1]
    half = own.shape[1]
    mine = pl.ds(pl.multiple_of(pair * half, half), half)
    other = pl.ds(pl.multiple_of((1 - pair) * half, half), half)
    back = dot(own[...], dw[:, mine], NT) + dot(oth[...], dw[:, other], NT)
    g_gate = (back * dgate_ref[...]).astype(BF16)
    g_up = (back * act_ref[...]).astype(BF16)
    grads_ref[:, :units] = g_gate
    grads_ref[:, units:2 * units] = g_up
    tail = split_columns(jnp.sum(back * hid_ref[...], axis=1, keepdims=True))
    grads_ref[:, 2 * units:] = tail
    send_ref[:, :half] = (dot(g_gate, gw[other, :], NT) + dot(g_up, uw[other, :], NT)).astype(BF16)
    send_ref[:, half:] = tail


def keep_body(sc, grads_ref, gw, uw, keep_ref):
    units = gw.shape[1]
    half = keep_ref.shape[1] - 128
    mine = pl.ds(pl.multiple_of(sc[1] * half, half), half)
    product = dot(grads_ref[:, :units], gw[mine, :], NT) + dot(grads_ref[:, units:2 * units], uw[mine, :], NT)
    keep_ref[:, :half] = product.astype(BF16)
    keep_ref[:, half:] = grads_ref[:, 2 * units:]


def split_columns(q):
    high = q.astype(BF16)
    low = (q - high.astype(F32)).astype(BF16)
    lane = lax.broadcasted_iota(jnp.int32, (q.shape[0], 128), 1)
    return jnp.where(lane == 0, high.astype(F32), jnp.where(lane == 1, low.astype(F32), 0.0)).astype(BF16)


def merge_body(experts, keep_ref, recv_ref, *outs):
    cap, wide = outs[0].shape
    half = wide - 128
    for m in range(experts):
        rows = slice(m * cap, (m + 1) * cap)
        outs[m][:, :half] = (keep_ref[rows, :half].astype(F32) + recv_ref[rows, :half].astype(F32)).astype(BF16)
        tail = keep_ref[rows, half:].astype(F32) + recv_ref[rows, half:].astype(F32)
        outs[m][:, half:] = split_columns(tail[:, 0:1] + tail[:, 1:2])


def combine_body(experts, cap, sc, routes_ref, probs_ref, *refs):
    parts, (out, gp_out) = refs[:experts], refs[experts:]
    half = out.shape[1]
    fanout = routes_ref.shape[0]
    found = picks(experts, cap, sc[0], routes_ref, probs_ref)
    total = None
    gp = [jnp.zeros((1, out.shape[0]), F32) for _ in range(fanout)]
    for m, (pick, _) in enumerate(found):
        rows = dot(pick, parts[m][:, :half], TN)
        total = rows if total is None else total + rows
        tail = dot(parts[m][:, half:], pick, TN)
        q = tail[0:1, :] + tail[1:2, :]
        for k in range(fanout):
            gp[k] = gp[k] + jnp.where(routes_ref[k:k + 1, :] == (sc[0] ^ m), q, 0.0)
    out[...] = total.astype(BF16)
    for k in range(fanout):
        gp_out[k:k + 1, :] = gp[k] / probs_ref[k:k + 1, :]


def on_device(tokens, grad_out, routes, gate_probs, gate_weight, up_weight, down_weight):
    count, half = tokens.shape
    fanout = routes.shape[1]
    experts = lax.axis_size("expert")
    groups = lax.axis_size("dp")
    units = gate_weight.shape[2]
    cap = 3 * count * fanout // (2 * experts)
    slots = experts * cap
    quarter = half // 2
    gw, uw, dw = gate_weight[0], up_weight[0], down_weight[0]
    me, pair, group = lax.axis_index("expert"), lax.axis_index("pair"), lax.axis_index("dp")
    scalars = jnp.stack([me, pair, group]).astype(jnp.int32)

    def swap(value):
        return lax.ppermute(value, "pair", [(0, 1), (1, 0)])

    def cross(values):
        return [values[0]] + [
            lax.ppermute(values[m], "expert", [(i, i ^ m) for i in range(experts)]) for m in range(1, experts)
        ]

    row_args = [routes.T, gate_probs.T]
    packed = call(
        functools.partial(pack_body, experts, cap),
        [struct((cap, half), BF16)] * (2 * experts),
        [*row_args, tokens, grad_out],
        scalars,
        hbm=(0, 1, 2, 3),
        scratch=(
            pltpu.VMEM((fanout, count), jnp.int32),
            pltpu.VMEM((fanout, count), F32),
            pltpu.VMEM((count, half), BF16),
            pltpu.VMEM((count, half), BF16),
            pltpu.SemaphoreType.DMA((4,)),
        ),
        vmem=PACK_VMEM,
    )

    def stack(values, after=()):
        return call(functools.partial(stack_body, experts), [struct((slots, half), BF16)], values, after=after)[0]

    x_parts = cross(packed[:experts])
    dy_parts = cross(packed[experts:])
    x_own, x_oth = stack(x_parts), stack([swap(v) for v in x_parts])

    square = struct((slots, units), F32)
    hid, hid_b, dgate, act = call(
        forward_body,
        [square, struct((slots, units), BF16), square, square],
        [x_own, x_oth, gw, uw],
        scalars,
    )
    dy_own, dy_oth = stack(dy_parts, [hid_b]), stack([swap(v) for v in dy_parts])

    first, second, third, fourth = call(
        weight_body,
        [struct((quarter, units), BF16)] * 2 + [struct((quarter, units), F32)] * 2,
        [dy_own, dy_oth, hid_b],
        scalars,
    )
    if groups == 4:
        from_near = lax.ppermute(first, "dp", [(0, 1), (1, 0), (2, 3), (3, 2)])
        from_end = lax.ppermute(second, "dp", [(0, 1), (3, 2)])
        from_mid = lax.ppermute(second, "dp", [(1, 2), (2, 1)])
        block = struct((quarter, units), F32)
        onward = call(onward_body, struct((quarter, units), BF16), [third, fourth, from_near], scalars)
        from_far = lax.ppermute(onward, "dp", [(0, 2), (2, 0), (1, 3), (3, 1)])
        part = call(partial_body, block, [third, fourth, from_near, from_end, from_mid], scalars)
    else:
        odd = group % 2 == 1
        first, second = first.astype(F32), second.astype(F32)
        whole = jnp.concatenate(
            [
                jnp.where(odd, first, third),
                jnp.where(odd, fourth, second),
                jnp.where(odd, second, fourth),
                jnp.where(odd, third, first),
            ],
            axis=0,
        )
        grad_down = lax.psum_scatter(whole[None], "dp", scatter_dimension=1, tiled=True)

    send, grads = call(
        backward_body,
        [struct((slots, half + 128), BF16), struct((slots, 2 * units + 128), BF16)],
        [dy_own, dy_oth, dw, gw, uw, hid, dgate, act],
        scalars,
        after=[second] if groups == 4 else [],
    )
    received = swap(send)
    keep = call(keep_body, struct((slots, half + 128), BF16), [grads, gw, uw], scalars)
    merged = call(functools.partial(merge_body, experts), [struct((cap, half + 128), BF16)] * experts, [keep, received])
    returned = cross(merged)
    grad_input, grad_probs = call(
        functools.partial(combine_body, experts, cap),
        [struct((count, half), BF16), struct((fanout, count), F32)],
        [*row_args, *returned],
        scalars,
    )

    if groups == 4:
        grad_down = call(total_body, block, [part, from_far], after=[grad_input])[None]

    return grad_input, grad_probs.T, grad_down


def solution(mesh):
    return jax.shard_map(
        on_device,
        mesh=mesh,
        in_specs=(
            P(("dp", "expert"), "pair"),
            P(("dp", "expert"), "pair"),
            P(("dp", "expert"), None),
            P(("dp", "expert"), None),
            P("expert", None, "pair"),
            P("expert", None, "pair"),
            P("expert", "pair", None),
        ),
        out_specs=(
            P(("dp", "expert"), "pair"),
            P(("dp", "expert"), None),
            P("expert", "dp", "pair"),
        ),
        check_vma=False,
    )
```

```python
import functools

import jax
import jax.numpy as jnp
from jax import lax
from jax.experimental import pallas as pl
from jax.experimental.pallas import tpu as pltpu
from jax.sharding import PartitionSpec as P

F32 = jnp.float32
BF16 = jnp.bfloat16
NT = (((1,), (1,)), ((), ()))
TN = (((0,), (0,)), ((), ()))
VMEM_LIMIT = 20 * 1024 * 1024
PACK_VMEM = 60 * 1024 * 1024


def dot(a, b, dims=(((1,), (0,)), ((), ()))):
    return lax.dot_general(a, b, dims, preferred_element_type=F32)


def call(body, out_shape, operands, located=False, after=(), hbm=(), scratch=(), vmem=VMEM_LIMIT):
    vm = pl.BlockSpec(memory_space=pltpu.VMEM)
    specs = [pl.BlockSpec(memory_space=pl.ANY)] * len(after)
    specs += [pl.BlockSpec(memory_space=pltpu.HBM) if i in hbm else vm for i in range(len(operands))]

    def run(*refs):
        place = [[lax.axis_index(axis) for axis in ("expert", "pair", "dp")]] if located else []
        body(*place, *refs[len(after):])

    return pl.pallas_call(
        run,
        out_shape=out_shape,
        in_specs=specs,
        out_specs=jax.tree.map(lambda _: vm, out_shape),
        scratch_shapes=list(scratch),
        compiler_params=pltpu.CompilerParams(vmem_limit_bytes=vmem),
    )(*after, *operands)


def struct(shape, dtype):
    return jax.ShapeDtypeStruct(shape, dtype)


def slot_rows(experts, me, routes_ref, probs_ref):
    fanout, count = routes_ref.shape
    routes = routes_ref[...]
    probs = probs_ref[...]
    row = lax.broadcasted_iota(jnp.int32, (8, count), 0)
    hits = jnp.zeros((8, count), F32)
    weights = jnp.zeros((8, count), F32)
    for k in range(fanout):
        same = routes[k:k + 1, :] == (row ^ me)
        hits = hits + jnp.where(same, 1.0, 0.0)
        weights = weights + jnp.where(same, probs[k:k + 1, :], 0.0)
    earlier = lax.broadcasted_iota(jnp.int32, (count, count), 0) < lax.broadcasted_iota(jnp.int32, (count, count), 1)
    before = dot(hits.astype(BF16), jnp.where(earlier, 1.0, 0.0).astype(BF16)).astype(jnp.int32)
    return hits, before, weights


def picks(experts, cap, me, routes_ref, probs_ref):
    hits, before, weights = slot_rows(experts, me, routes_ref, probs_ref)
    slot = lax.broadcasted_iota(jnp.int32, (cap, hits.shape[1]), 0)
    found = []
    for m in range(experts):
        chosen = (slot == before[m:m + 1, :]) & (hits[m:m + 1, :] > 0.5)
        pick = jnp.where(chosen, 1.0, 0.0)
        found.append((pick.astype(BF16), jnp.sum(pick * weights[m:m + 1, :], axis=1, keepdims=True)))
    return found


def pack_body(experts, cap, sc, routes_hbm, probs_hbm, tok_hbm, dy_hbm, *rest):
    x_out, dy_out = rest[:experts], rest[experts:2 * experts]
    routes_ref, probs_ref, tok_ref, dy_ref, sems = rest[2 * experts:]
    copies = [
        pltpu.make_async_copy(source, target, sems.at[i])
        for i, (source, target) in enumerate(
            [(routes_hbm, routes_ref), (probs_hbm, probs_ref), (tok_hbm, tok_ref), (dy_hbm, dy_ref)]
        )
    ]
    for copy in copies:
        copy.start()
    copies[0].wait()
    copies[1].wait()
    found = picks(experts, cap, sc[0], routes_ref, probs_ref)
    copies[2].wait()
    tok = tok_ref[...]
    for m, (pick, _) in enumerate(found):
        x_out[m][...] = dot(pick, tok).astype(BF16)
    copies[3].wait()
    dy = dy_ref[...]
    for m, (pick, p_col) in enumerate(found):
        dy_out[m][...] = (p_col * dot(pick, dy)).astype(BF16)


def copy_body(ref, out):
    out[...] = ref[...]


def load_body(gw, uw, out):
    units = gw.shape[1]
    out[:, :units] = gw[...]
    out[:, units:] = uw[...]


def stack_body(count, *refs):
    blocks, outs = refs[:count], refs[count:]
    cap = blocks[0].shape[0]
    for m, ref in enumerate(blocks):
        rows = slice(m * cap, (m + 1) * cap)
        low = 0
        for out in outs:
            out[rows, :] = ref[:, low:low + out.shape[1]]
            low += out.shape[1]


def forward_body(sc, own, oth, w, hid_ref, hid_b_ref, dgate_ref, act_ref):
    pair = sc[1]
    half = own.shape[1]
    mine = pl.ds(pl.multiple_of(pair * half, half), half)
    other = pl.ds(pl.multiple_of((1 - pair) * half, half), half)
    both = dot(own[...], w[mine, :]) + dot(oth[...], w[other, :])
    units = w.shape[1] // 2
    gate, up = both[:, :units], both[:, units:]
    sig = jax.nn.sigmoid(gate)
    act = gate * sig
    hid = act * up
    hid_ref[...] = hid
    hid_b_ref[...] = hid.astype(BF16)
    dgate_ref[...] = up * sig * (1.0 + gate * (1.0 - sig))
    act_ref[...] = act


def weight_body(which, sc, own, oth, hid_b, *outs):
    group, pair = sc[2], sc[1]
    quarter = own.shape[1] // 2
    odd = group % 2
    hid = hid_b[...]

    def block(out, mine, index):
        columns = pl.ds(pl.multiple_of(index * quarter, quarter), quarter)

        @pl.when(mine)
        def _():
            out[...] = dot(own[:, columns], hid, TN).astype(out.dtype)

        @pl.when(jnp.logical_not(mine))
        def _():
            out[...] = dot(oth[:, columns], hid, TN).astype(out.dtype)

    same = pair == odd
    differ = jnp.logical_not(same)
    places = [(differ, 1 - odd), (same, 1 - odd), (same, odd), (differ, odd)]
    for out, index in zip(outs, which):
        block(out, *places[index])


def onward_body(sc, third, fourth, near, out):
    inner = (sc[2] == 1) | (sc[2] == 2)

    @pl.when(inner)
    def _():
        out[...] = (third[...] + near[...].astype(F32)).astype(BF16)

    @pl.when(jnp.logical_not(inner))
    def _():
        out[...] = fourth[...].astype(BF16)


def partial_body(sc, third, fourth, near, end, mid, out):
    inner = (sc[2] == 1) | (sc[2] == 2)

    @pl.when(inner)
    def _():
        out[...] = fourth[...] + mid[...].astype(F32) + end[...].astype(F32)

    @pl.when(jnp.logical_not(inner))
    def _():
        out[...] = third[...] + near[...].astype(F32)


def backward_body(sc, own, oth, dw, gw, uw, hid_ref, dgate_ref, act_ref, grads_ref, *send):
    pair = sc[1]
    units = hid_ref.shape[1]
    half = own.shape[1]
    mine = pl.ds(pl.multiple_of(pair * half, half), half)
    other = pl.ds(pl.multiple_of((1 - pair) * half, half), half)
    back = dot(own[...], dw[:, mine], NT) + dot(oth[...], dw[:, other], NT)
    g_gate = (back * dgate_ref[...]).astype(BF16)
    g_up = (back * act_ref[...]).astype(BF16)
    grads_ref[:, :units] = g_gate
    grads_ref[:, units:2 * units] = g_up
    tail = split_columns(jnp.sum(back * hid_ref[...], axis=1, keepdims=True))
    grads_ref[:, 2 * units:] = tail
    product = (dot(g_gate, gw[other, :], NT) + dot(g_up, uw[other, :], NT)).astype(BF16)
    cap = send[0].shape[0]
    for m, ref in enumerate(send):
        rows = slice(m * cap, (m + 1) * cap)
        ref[:, :half] = product[rows]
        ref[:, half:] = tail[rows]


def keep_body(sc, grads_ref, gw, uw, keep_ref):
    units = gw.shape[1]
    half = keep_ref.shape[1] - 128
    mine = pl.ds(pl.multiple_of(sc[1] * half, half), half)
    product = (
        dot(grads_ref[:, :units], gw[mine, :], NT) + dot(grads_ref[:, units:2 * units], uw[mine, :], NT)
    )
    keep_ref[:, :half] = product.astype(BF16)
    keep_ref[:, half:] = grads_ref[:, 2 * units:]


def split_columns(q):
    high = q.astype(BF16)
    low = (q - high.astype(F32)).astype(BF16)
    lane = lax.broadcasted_iota(jnp.int32, (q.shape[0], 128), 1)
    return jnp.where(lane == 0, high.astype(F32), jnp.where(lane == 1, low.astype(F32), 0.0)).astype(BF16)


def merge_body(experts, keep_ref, *refs):
    received, outs = refs[:experts], refs[experts:]
    cap, wide = outs[0].shape
    half = wide - 128
    for m in range(experts):
        rows = slice(m * cap, (m + 1) * cap)
        outs[m][:, :half] = (keep_ref[rows, :half].astype(F32) + received[m][:, :half].astype(F32)).astype(BF16)
        tail = keep_ref[rows, half:].astype(F32) + received[m][:, half:].astype(F32)
        outs[m][:, half:] = split_columns(tail[:, 0:1] + tail[:, 1:2])


def combine_body(experts, cap, sc, routes_ref, probs_ref, *refs):
    parts, (out, gp_out) = refs[:experts], refs[experts:]
    half = out.shape[1]
    fanout = routes_ref.shape[0]
    found = picks(experts, cap, sc[0], routes_ref, probs_ref)
    total = None
    gp = [jnp.zeros((1, out.shape[0]), F32) for _ in range(fanout)]
    for m, (pick, _) in enumerate(found):
        rows = dot(pick, parts[m][:, :half], TN)
        total = rows if total is None else total + rows
        tail = dot(parts[m][:, half:], pick, TN)
        q = tail[0:1, :] + tail[1:2, :]
        for k in range(fanout):
            gp[k] = gp[k] + jnp.where(routes_ref[k:k + 1, :] == (sc[0] ^ m), q, 0.0)
    out[...] = total.astype(BF16)
    for k in range(fanout):
        gp_out[k:k + 1, :] = gp[k] / probs_ref[k:k + 1, :]


def on_device(tokens, grad_out, routes, gate_probs, gate_weight, up_weight, down_weight):
    count, half = tokens.shape
    fanout = routes.shape[1]
    experts = lax.axis_size("expert")
    groups = lax.axis_size("dp")
    units = gate_weight.shape[2]
    cap = 3 * count * fanout // (2 * experts)
    slots = experts * cap
    quarter = half // 2
    gw, uw, dw = gate_weight[0], up_weight[0], down_weight[0]
    group = lax.axis_index("dp")

    def swap(value):
        return lax.ppermute(value, "pair", [(0, 1), (1, 0)])

    def cross(values):
        return [values[0]] + [
            lax.ppermute(values[m], "expert", [(i, i ^ m) for i in range(experts)]) for m in range(1, experts)
        ]

    row_args = [routes.T, gate_probs.T]
    packed = call(
        functools.partial(pack_body, experts, cap),
        [struct((cap, half), BF16)] * (2 * experts),
        [*row_args, tokens, grad_out],
        located=True,
        hbm=(0, 1, 2, 3),
        scratch=(
            pltpu.VMEM((fanout, count), jnp.int32),
            pltpu.VMEM((fanout, count), F32),
            pltpu.VMEM((count, half), BF16),
            pltpu.VMEM((count, half), BF16),
            pltpu.SemaphoreType.DMA((4,)),
        ),
        vmem=PACK_VMEM,
    )

    def stack(values, after=()):
        return call(functools.partial(stack_body, experts), [struct((slots, half), BF16)], values, after=after)[0]

    x_parts = cross(packed[:experts])
    dy_parts = cross(packed[experts:])
    (w_all,) = call(load_body, [struct((gw.shape[0], 2 * units), BF16)], [gw, uw])
    x_parts[0] = call(copy_body, struct((cap, half), BF16), [x_parts[0]], after=[w_all])
    x_own, x_oth = stack(x_parts), stack([swap(v) for v in x_parts])

    square = struct((slots, units), F32)
    hid, hid_b, dgate, act = call(
        forward_body,
        [square, struct((slots, units), BF16), square, square],
        [x_own, x_oth, w_all],
        located=True,
    )
    dy_own, dy_oth = stack(dy_parts, [hid_b]), stack([swap(v) for v in dy_parts])

    blocks = [struct((quarter, units), t) for t in (BF16, BF16, F32, F32)]
    w_args = [dy_own, dy_oth, hid_b]
    first, second = call(functools.partial(weight_body, [0, 1]), blocks[:2], w_args, located=True)
    third, fourth = call(functools.partial(weight_body, [2, 3]), blocks[2:], w_args, located=True, after=[first])
    if groups == 4:
        from_near = lax.ppermute(first, "dp", [(0, 1), (1, 0), (2, 3), (3, 2)])
        from_end = lax.ppermute(second, "dp", [(0, 1), (3, 2)])
        from_mid = lax.ppermute(second, "dp", [(1, 2), (2, 1)])
        arrived_mid, arrived_end = [from_mid], [from_end]
        onward = call(onward_body, struct((quarter, units), BF16), [third, fourth, from_near], located=True)
        from_far = lax.ppermute(onward, "dp", [(0, 2), (2, 0), (1, 3), (3, 1)])
        part = call(partial_body, struct((quarter, units), F32), [third, fourth, from_near, from_end, from_mid], located=True)
    else:
        arrived_mid, arrived_end = [], []
        odd = group % 2 == 1
        first, second = first.astype(F32), second.astype(F32)
        whole = jnp.concatenate(
            [
                jnp.where(odd, first, third),
                jnp.where(odd, fourth, second),
                jnp.where(odd, second, fourth),
                jnp.where(odd, third, first),
            ],
            axis=0,
        )
        grad_down = lax.psum_scatter(whole[None], "dp", scatter_dimension=1, tiled=True)

    grads, *send = call(
        backward_body,
        [struct((slots, 2 * units + 128), BF16)] + [struct((cap, half + 128), BF16)] * experts,
        [dy_own, dy_oth, dw, gw, uw, hid, dgate, act],
        located=True,
        after=[second],
    )
    received = [swap(v) for v in send]
    keep = call(keep_body, struct((slots, half + 128), BF16), [grads, gw, uw], located=True, after=arrived_mid)
    merged = call(functools.partial(merge_body, experts), [struct((cap, half + 128), BF16)] * experts, [keep, *received], after=arrived_end)
    returned = cross(merged)
    grad_input, grad_probs = call(
        functools.partial(combine_body, experts, cap),
        [struct((count, half), BF16), struct((fanout, count), F32)],
        [*row_args, *returned],
        located=True,
    )

    if groups == 4:
        grad_down = (part + from_far.astype(F32))[None]
    return grad_input, grad_probs.T, grad_down


def solution(mesh):
    return jax.shard_map(
        on_device,
        mesh=mesh,
        in_specs=(
            P(("dp", "expert"), "pair"),
            P(("dp", "expert"), "pair"),
            P(("dp", "expert"), None),
            P(("dp", "expert"), None),
            P("expert", None, "pair"),
            P("expert", None, "pair"),
            P("expert", "pair", None),
        ),
        out_specs=(
            P(("dp", "expert"), "pair"),
            P(("dp", "expert"), None),
            P("expert", "dp", "pair"),
        ),
        check_vma=False,
    )
```

```python
import functools

import jax
import jax.numpy as jnp
from jax import lax
from jax.experimental import pallas as pl
from jax.experimental.pallas import tpu as pltpu
from jax.sharding import PartitionSpec as P

F32 = jnp.float32
BF16 = jnp.bfloat16
NT = (((1,), (1,)), ((), ()))
TN = (((0,), (0,)), ((), ()))
VMEM_LIMIT = 20 * 1024 * 1024
PACK_VMEM = 60 * 1024 * 1024


def dot(a, b, dims=(((1,), (0,)), ((), ()))):
    return lax.dot_general(a, b, dims, preferred_element_type=F32)


def call(body, out_shape, operands, located=False, after=(), hbm=(), scratch=(), vmem=VMEM_LIMIT):
    vm = pl.BlockSpec(memory_space=pltpu.VMEM)
    specs = [pl.BlockSpec(memory_space=pl.ANY)] * len(after)
    specs += [pl.BlockSpec(memory_space=pltpu.HBM) if i in hbm else vm for i in range(len(operands))]

    def run(*refs):
        place = [[lax.axis_index(axis) for axis in ("expert", "pair", "dp")]] if located else []
        body(*place, *refs[len(after):])

    return pl.pallas_call(
        run,
        out_shape=out_shape,
        in_specs=specs,
        out_specs=jax.tree.map(lambda _: vm, out_shape),
        scratch_shapes=list(scratch),
        compiler_params=pltpu.CompilerParams(vmem_limit_bytes=vmem),
    )(*after, *operands)


def struct(shape, dtype):
    return jax.ShapeDtypeStruct(shape, dtype)


def slot_rows(experts, me, routes_ref, probs_ref):
    fanout, count = routes_ref.shape
    routes = routes_ref[...]
    probs = probs_ref[...]
    row = lax.broadcasted_iota(jnp.int32, (8, count), 0)
    hits = jnp.zeros((8, count), F32)
    weights = jnp.zeros((8, count), F32)
    for k in range(fanout):
        same = routes[k:k + 1, :] == (row ^ me)
        hits = hits + jnp.where(same, 1.0, 0.0)
        weights = weights + jnp.where(same, probs[k:k + 1, :], 0.0)
    earlier = lax.broadcasted_iota(jnp.int32, (count, count), 0) < lax.broadcasted_iota(jnp.int32, (count, count), 1)
    before = dot(hits.astype(BF16), jnp.where(earlier, 1.0, 0.0).astype(BF16)).astype(jnp.int32)
    return hits, before, weights


def picks(experts, cap, me, routes_ref, probs_ref):
    hits, before, weights = slot_rows(experts, me, routes_ref, probs_ref)
    slot = lax.broadcasted_iota(jnp.int32, (cap, hits.shape[1]), 0)
    found = []
    for m in range(experts):
        chosen = (slot == before[m:m + 1, :]) & (hits[m:m + 1, :] > 0.5)
        pick = jnp.where(chosen, 1.0, 0.0)
        found.append((pick.astype(BF16), jnp.sum(pick * weights[m:m + 1, :], axis=1, keepdims=True)))
    return found


def pack_body(experts, cap, sc, routes_hbm, probs_hbm, tok_hbm, dy_hbm, *rest):
    x_out, dy_out = rest[:experts], rest[experts:2 * experts]
    routes_ref, probs_ref, tok_ref, dy_ref, sems = rest[2 * experts:]
    copies = [
        pltpu.make_async_copy(source, target, sems.at[i])
        for i, (source, target) in enumerate(
            [(routes_hbm, routes_ref), (probs_hbm, probs_ref), (tok_hbm, tok_ref), (dy_hbm, dy_ref)]
        )
    ]
    for copy in copies:
        copy.start()
    copies[0].wait()
    copies[1].wait()
    found = picks(experts, cap, sc[0], routes_ref, probs_ref)
    copies[2].wait()
    tok = tok_ref[...]
    for m, (pick, _) in enumerate(found):
        x_out[m][...] = dot(pick, tok).astype(BF16)
    copies[3].wait()
    dy = dy_ref[...]
    for m, (pick, p_col) in enumerate(found):
        dy_out[m][...] = (p_col * dot(pick, dy)).astype(BF16)


def copy_body(ref, out):
    out[...] = ref[...]


def load_body(gw, uw, out):
    units = gw.shape[1]
    out[:, :units] = gw[...]
    out[:, units:] = uw[...]


def stack_body(count, *refs):
    blocks, outs = refs[:count], refs[count:]
    cap = blocks[0].shape[0]
    for m, ref in enumerate(blocks):
        rows = slice(m * cap, (m + 1) * cap)
        low = 0
        for out in outs:
            out[rows, :] = ref[:, low:low + out.shape[1]]
            low += out.shape[1]


def forward_body(sc, own, oth, w, hid_ref, hid_b_ref, dgate_ref, act_ref):
    pair = sc[1]
    half = own.shape[1]
    mine = pl.ds(pl.multiple_of(pair * half, half), half)
    other = pl.ds(pl.multiple_of((1 - pair) * half, half), half)
    both = dot(own[...], w[mine, :]) + dot(oth[...], w[other, :])
    units = w.shape[1] // 2
    gate, up = both[:, :units], both[:, units:]
    sig = jax.nn.sigmoid(gate)
    act = gate * sig
    hid = act * up
    hid_ref[...] = hid
    hid_b_ref[...] = hid.astype(BF16)
    dgate_ref[...] = up * sig * (1.0 + gate * (1.0 - sig))
    act_ref[...] = act


def each_block(sc, own, oth, index, emit):
    pair, odd = sc[1], sc[2] % 2
    quarter = own.shape[1] // 2
    flip = (0, 1, 1, 0)[index]
    mine = (pair == odd) if flip else (pair != odd)
    half = (1 - odd) if index < 2 else odd
    columns = pl.ds(pl.multiple_of(half * quarter, quarter), quarter)

    @pl.when(mine)
    def _():
        emit(own[:, columns])

    @pl.when(jnp.logical_not(mine))
    def _():
        emit(oth[:, columns])


def weight_body(which, sc, own, oth, hid_b, *outs):
    for out, index in zip(outs, which):
        def emit(rows, out=out):
            out[...] = dot(rows, hid_b[...], TN).astype(out.dtype)

        each_block(sc, own, oth, index, emit)


def onward_body(sc, own, oth, hid_b, near, out):
    inner = (sc[2] == 1) | (sc[2] == 2)

    @pl.when(inner)
    def _():
        def emit(rows):
            out[...] = (dot(rows, hid_b[...], TN) + near[...].astype(F32)).astype(BF16)

        each_block(sc, own, oth, 2, emit)

    @pl.when(jnp.logical_not(inner))
    def _():
        def emit(rows):
            out[...] = dot(rows, hid_b[...], TN).astype(BF16)

        each_block(sc, own, oth, 3, emit)


def partial_body(sc, own, oth, hid_b, near, end, mid, out):
    inner = (sc[2] == 1) | (sc[2] == 2)

    @pl.when(inner)
    def _():
        def emit(rows):
            out[...] = dot(rows, hid_b[...], TN) + (mid[...].astype(F32) + end[...].astype(F32))

        each_block(sc, own, oth, 3, emit)

    @pl.when(jnp.logical_not(inner))
    def _():
        def emit(rows):
            out[...] = dot(rows, hid_b[...], TN) + near[...].astype(F32)

        each_block(sc, own, oth, 2, emit)


def backward_body(sc, own, oth, dw, gw, uw, hid_ref, dgate_ref, act_ref, grads_ref, *send):
    pair = sc[1]
    units = hid_ref.shape[1]
    half = own.shape[1]
    mine = pl.ds(pl.multiple_of(pair * half, half), half)
    other = pl.ds(pl.multiple_of((1 - pair) * half, half), half)
    back = dot(own[...], dw[:, mine], NT) + dot(oth[...], dw[:, other], NT)
    g_gate = (back * dgate_ref[...]).astype(BF16)
    g_up = (back * act_ref[...]).astype(BF16)
    grads_ref[:, :units] = g_gate
    grads_ref[:, units:2 * units] = g_up
    tail = split_columns(jnp.sum(back * hid_ref[...], axis=1, keepdims=True))
    grads_ref[:, 2 * units:] = tail
    product = (dot(g_gate, gw[other, :], NT) + dot(g_up, uw[other, :], NT)).astype(BF16)
    cap = send[0].shape[0]
    for m, ref in enumerate(send):
        rows = slice(m * cap, (m + 1) * cap)
        ref[:, :half] = product[rows]
        ref[:, half:] = tail[rows]


def keep_body(sc, grads_ref, gw, uw, keep_ref):
    units = gw.shape[1]
    half = keep_ref.shape[1] - 128
    mine = pl.ds(pl.multiple_of(sc[1] * half, half), half)
    product = (
        dot(grads_ref[:, :units], gw[mine, :], NT) + dot(grads_ref[:, units:2 * units], uw[mine, :], NT)
    )
    keep_ref[:, :half] = product.astype(BF16)
    keep_ref[:, half:] = grads_ref[:, 2 * units:]


def split_columns(q):
    high = q.astype(BF16)
    low = (q - high.astype(F32)).astype(BF16)
    lane = lax.broadcasted_iota(jnp.int32, (q.shape[0], 128), 1)
    return jnp.where(lane == 0, high.astype(F32), jnp.where(lane == 1, low.astype(F32), 0.0)).astype(BF16)


def merge_body(experts, keep_ref, *refs):
    received, outs = refs[:experts], refs[experts:]
    cap, wide = outs[0].shape
    half = wide - 128
    for m in range(experts):
        rows = slice(m * cap, (m + 1) * cap)
        outs[m][:, :half] = (keep_ref[rows, :half].astype(F32) + received[m][:, :half].astype(F32)).astype(BF16)
        tail = keep_ref[rows, half:].astype(F32) + received[m][:, half:].astype(F32)
        outs[m][:, half:] = split_columns(tail[:, 0:1] + tail[:, 1:2])


def combine_body(experts, cap, sc, routes_ref, probs_ref, *refs):
    parts, (out, gp_out) = refs[:experts], refs[experts:]
    half = out.shape[1]
    fanout = routes_ref.shape[0]
    found = picks(experts, cap, sc[0], routes_ref, probs_ref)
    total = None
    gp = [jnp.zeros((1, out.shape[0]), F32) for _ in range(fanout)]
    for m, (pick, _) in enumerate(found):
        rows = dot(pick, parts[m][:, :half], TN)
        total = rows if total is None else total + rows
        tail = dot(parts[m][:, half:], pick, TN)
        q = tail[0:1, :] + tail[1:2, :]
        for k in range(fanout):
            gp[k] = gp[k] + jnp.where(routes_ref[k:k + 1, :] == (sc[0] ^ m), q, 0.0)
    out[...] = total.astype(BF16)
    for k in range(fanout):
        gp_out[k:k + 1, :] = gp[k] / probs_ref[k:k + 1, :]


def on_device(tokens, grad_out, routes, gate_probs, gate_weight, up_weight, down_weight):
    count, half = tokens.shape
    fanout = routes.shape[1]
    experts = lax.axis_size("expert")
    groups = lax.axis_size("dp")
    units = gate_weight.shape[2]
    cap = 3 * count * fanout // (2 * experts)
    slots = experts * cap
    quarter = half // 2
    gw, uw, dw = gate_weight[0], up_weight[0], down_weight[0]
    group = lax.axis_index("dp")

    def swap(value):
        return lax.ppermute(value, "pair", [(0, 1), (1, 0)])

    def cross(values):
        return [values[0]] + [
            lax.ppermute(values[m], "expert", [(i, i ^ m) for i in range(experts)]) for m in range(1, experts)
        ]

    row_args = [routes.T, gate_probs.T]
    packed = call(
        functools.partial(pack_body, experts, cap),
        [struct((cap, half), BF16)] * (2 * experts),
        [*row_args, tokens, grad_out],
        located=True,
        hbm=(0, 1, 2, 3),
        scratch=(
            pltpu.VMEM((fanout, count), jnp.int32),
            pltpu.VMEM((fanout, count), F32),
            pltpu.VMEM((count, half), BF16),
            pltpu.VMEM((count, half), BF16),
            pltpu.SemaphoreType.DMA((4,)),
        ),
        vmem=PACK_VMEM,
    )

    def stack(values, after=()):
        return call(functools.partial(stack_body, experts), [struct((slots, half), BF16)], values, after=after)[0]

    x_parts = cross(packed[:experts])
    dy_parts = cross(packed[experts:])
    (w_all,) = call(load_body, [struct((gw.shape[0], 2 * units), BF16)], [gw, uw], after=[x_parts[1]])
    x_parts[0] = call(copy_body, struct((cap, half), BF16), [x_parts[0]], after=[w_all])
    x_own, x_oth = stack(x_parts), stack([swap(v) for v in x_parts])

    square = struct((slots, units), F32)
    hid, hid_b, dgate, act = call(
        forward_body,
        [square, struct((slots, units), BF16), square, square],
        [x_own, x_oth, w_all],
        located=True,
    )
    dy_own = stack(dy_parts, [hid_b])
    dy_oth = stack([swap(v) for v in dy_parts])

    blocks = [struct((quarter, units), t) for t in (BF16, BF16, F32, F32)]
    w_args = [dy_own, dy_oth, hid_b]

    def weights(index):
        return call(functools.partial(weight_body, index), [blocks[i] for i in index], w_args, located=True)

    first, second = weights([0, 1])
    if groups != 4:
        third, fourth = weights([2, 3])

    grads, *send = call(
        backward_body,
        [struct((slots, 2 * units + 128), BF16)] + [struct((cap, half + 128), BF16)] * experts,
        [dy_own, dy_oth, dw, gw, uw, hid, dgate, act],
        located=True,
        after=[second],
    )
    received = [swap(v) for v in send]
    arrived_mid, arrived_end = [], []
    if groups == 4:
        from_near = lax.ppermute(first, "dp", [(0, 1), (1, 0), (2, 3), (3, 2)])
        from_end = lax.ppermute(second, "dp", [(0, 1), (3, 2)])
        from_mid = lax.ppermute(second, "dp", [(1, 2), (2, 1)])
        arrived_mid, arrived_end = [from_mid], [from_end]
        onward = call(onward_body, struct((quarter, units), BF16), [*w_args, from_near], located=True)
        from_far = lax.ppermute(onward, "dp", [(0, 2), (2, 0), (1, 3), (3, 1)])
        part = call(partial_body, struct((quarter, units), F32), [*w_args, from_near, from_end, from_mid], located=True)
    else:
        odd = group % 2 == 1
        first, second = first.astype(F32), second.astype(F32)
        whole = jnp.concatenate(
            [
                jnp.where(odd, first, third),
                jnp.where(odd, fourth, second),
                jnp.where(odd, second, fourth),
                jnp.where(odd, third, first),
            ],
            axis=0,
        )
        grad_down = lax.psum_scatter(whole[None], "dp", scatter_dimension=1, tiled=True)

    keep = call(keep_body, struct((slots, half + 128), BF16), [grads, gw, uw], located=True, after=arrived_mid)
    merged = call(functools.partial(merge_body, experts), [struct((cap, half + 128), BF16)] * experts, [keep, *received])
    returned = cross(merged)
    grad_input, grad_probs = call(
        functools.partial(combine_body, experts, cap),
        [struct((count, half), BF16), struct((fanout, count), F32)],
        [*row_args, *returned],
        located=True,
        after=arrived_end,
    )

    if groups == 4:
        grad_down = (part + from_far.astype(F32))[None]
    return grad_input, grad_probs.T, grad_down


def solution(mesh):
    return jax.shard_map(
        on_device,
        mesh=mesh,
        in_specs=(
            P(("dp", "expert"), "pair"),
            P(("dp", "expert"), "pair"),
            P(("dp", "expert"), None),
            P(("dp", "expert"), None),
            P("expert", None, "pair"),
            P("expert", None, "pair"),
            P("expert", "pair", None),
        ),
        out_specs=(
            P(("dp", "expert"), "pair"),
            P(("dp", "expert"), None),
            P("expert", "dp", "pair"),
        ),
        check_vma=False,
    )
```
